32 devices in a mesh: pipe: 4 (over x, core), expert: 8 (over z, y).
Axes of the slice: x: 2, y: 2, z: 4, core: 2. Of those that a mesh axis runs over, the one named last changes fastest.
Arguments:
- held: bfloat16 [4, 256, 2048], P('pipe', 'expert'), may hold values from -23 to 23
- fresh: bfloat16 [256, 2048], P('expert'), may hold values from -23 to 23
- routes: int32 [4, 256, 2], P('pipe', 'expert'), may hold values from 0 to 7, all different within a row; in each aligned block of 32 rows (0 to 31, 32 to 63, ..., all dimensions but the last counted through in order) at most 16 rows name the same one
- norm_gain: float32 [4, 2048], P('pipe'), may hold values from 0.25 to 1.75
- router: bfloat16 [4, 2048, 8], P('pipe'), may hold values from -0.125 to 0.125
- w_gate: bfloat16 [4, 8, 2048, 7168], P('pipe', 'expert'), may hold values from -0.125 to 0.125
- w_up: bfloat16 [4, 8, 2048, 7168], P('pipe', 'expert'), may hold values from -0.125 to 0.125
- w_down: bfloat16 [4, 8, 7168, 2048], P('pipe', 'expert'), may hold values from -0.0625 to 0.0625
Outputs:
- section_out: bfloat16 [4, 256, 2048], P('pipe', 'expert')
The draws below stay inside these ranges and needn't reach their ends.
Inputs may be any that keep to these rules, and one draw needn't show every extreme that they name: `routes`: each token names two different experts; among the 32 tokens of one device at one section no expert is named more than 16 times, and in every draw some device's tokens name one expert exactly 16 times.
All inputs are finite; a program needn't handle non-finite values.
Results may differ from the reference program's by a relative error of at most 0.0045.
Values may be sent and summed in bfloat16 or wider, within the bound.
No kernel may reach another device: no remote copies, remote signals or barrier semaphores. Data moves between devices by JAX's collectives and lax.ppermute only.
A program may use at most 128 MiB of HBM per device.

```python
import math
import jax
import jax.numpy as jnp
import numpy as np
from jax import lax

D = 2048
FF = 7168
EXPERTS = 8
TOP = 2
TOK_DEV = 32
SECTIONS = 4
SHARDS = 1
HID_DEV = 7168
CAP = 16
TOKENS = 256
N_EXPERT = 8


def scaled_rows(key, row_count):
    key_base = jax.random.fold_in(key, 11)
    key_rows = jax.random.fold_in(key, 12)
    key_cols = jax.random.fold_in(key, 13)
    base_draw = jnp.clip(jax.random.normal(key_base, (row_count, D), jnp.float32), -5.0, 5.0)
    row_scale = jnp.exp(jax.random.uniform(key_rows, (row_count, 1), jnp.float32, -0.92, 0.92))
    col_scale = jnp.exp(jax.random.uniform(key_cols, (1, D), jnp.float32, -0.6, 0.6))
    return base_draw * row_scale * col_scale


def draw_held(key, part):
    values = scaled_rows(jax.random.fold_in(key, 1), SECTIONS * TOKENS)
    return values.reshape(SECTIONS, TOKENS, D).astype(jnp.bfloat16)


def draw_fresh(key, part):
    return scaled_rows(jax.random.fold_in(key, 2), TOKENS).astype(jnp.bfloat16)


def shard_levels(own_key, shape, shards, low, largest):
    factor_of, own = 1.0, jax.random.fold_in(own_key, 6)
    for dim, shards_of in shards:
        heights = jnp.exp(jax.random.uniform(jax.random.fold_in(own, dim), (shards_of,), jnp.float32, low / len(shards), largest / len(shards)))
        factor_of = factor_of * jnp.repeat(heights, shape[dim] // shards_of).reshape([-1 if axis == dim else 1 for axis in range(len(shape))])
    return factor_of


def deal_out(stream_key, own, number, rows, number_of, top, reach, slope):
    sequence = jax.random.permutation(stream_key, number_of)
    packed, usual = load_shares(number_of, rows * top, reach, slope, True), load_shares(number_of, rows * top, reach, slope, False)
    places = jnp.arange(number_of)

    def named(lengths, rotation):
        used = int((lengths > 0).sum())
        fixed = max(1, used // 4)
        shifted = fixed + (places - fixed + rotation * (used - fixed)) % max(1, number_of - fixed)
        return jnp.zeros((number_of,), jnp.int32).at[sequence[jnp.where(places < fixed, places, shifted)]].set(jnp.asarray(lengths, jnp.int32))

    lengths = jnp.where(number % 4 == 0, named(packed, number // 4), named(usual, number - number // 4 - 1))
    mixed = jax.random.permutation(jax.random.fold_in(own, 3), number_of)
    donor, receiver = mixed[0:number_of // 2 * 2:2], mixed[1:number_of // 2 * 2:2]
    room = jnp.minimum(lengths[donor] - 1, reach - lengths[receiver]) // 2
    room = jnp.where((donor == sequence[0]) | (receiver == sequence[0]) | (lengths[receiver] == 0), 0, jnp.maximum(room, 0))
    shifted = jax.random.randint(jax.random.fold_in(own, 4), (number_of // 2,), 0, 1 << 20) % (room + 1)
    lengths = lengths.at[donor].add(-shifted).at[receiver].add(shifted)
    members = jnp.searchsorted(jnp.cumsum(lengths), jnp.arange(rows * top), side="right").astype(jnp.int32)
    grid = members.reshape(top, rows).T
    grid = grid[jax.random.permutation(jax.random.fold_in(own, 1), rows)]
    rotation = jax.random.randint(jax.random.fold_in(own, 2), (rows, 1), 0, top)
    return jnp.take_along_axis(grid, (jnp.arange(top)[None, :] + rotation) % top, axis=1)


def load_shares(count, total, reach, lean, full):
    weights = [(1 << 20) // math.isqrt(grade ** lean) + 1 for grade in range(1, count + 1)]
    largest = reach if full else min(reach, max(-(-total // count), total * weights[0] // sum(weights)))
    least = 1 if total - largest >= count - 1 else 0
    counts, surplus = [largest] + [least] * (count - 1), total - largest - least * (count - 1)
    while surplus > 0:
        candidates = [i for i in range(1, count) if counts[i] < largest] or [i for i in range(1, count) if counts[i] < reach]
        whole, budget = sum([weights[i] for i in candidates]), surplus
        for i in candidates:
            addition = min(reach - counts[i], max(1, budget * weights[i] // whole), surplus)
            counts[i] = counts[i] + addition
            surplus = surplus - addition
    return np.array(counts)


def centred(own_key, shape, deviation, bound, pieces=(), kind=jnp.bfloat16):
    values = jax.random.normal(own_key, shape, jnp.float32) * deviation
    if len(pieces) > 0:
        values = shard_levels(own_key, shape, pieces, -0.22, 0.18) * values
    return jnp.clip(values, min=-bound, max=bound).astype(kind)


def setup_inputs(seed: int = 0) -> dict:
    key_list = jax.random.split(jax.random.key(seed), 9)
    held = draw_held(jax.random.fold_in(key_list[8], 71), 0)
    fresh = draw_fresh(jax.random.fold_in(key_list[8], 71), 0)
    routes_keys = jax.random.split(jax.random.fold_in(key_list[2], 1), SECTIONS * TOKENS // TOK_DEV)
    routes_turns = jax.random.permutation(jax.random.fold_in(key_list[2], 3), SECTIONS * TOKENS // TOK_DEV)
    routes = jax.vmap(lambda own, number: deal_out(jax.random.fold_in(key_list[2], 2), own, number, TOK_DEV, EXPERTS, TOP, CAP, 2))(routes_keys, routes_turns).reshape((SECTIONS, TOKENS, TOP))
    norm_gain = jnp.clip(1.0 + 0.15 * jax.random.normal(key_list[3], (SECTIONS, D), jnp.float32), 0.25, 1.75)
    router = centred(key_list[4], (SECTIONS, D, EXPERTS), D ** -0.5, 0.125, ((0, 4),))
    w_gate = centred(key_list[5], (SECTIONS, N_EXPERT, D, HID_DEV), D ** -0.5, 0.125, ((0, 4), (1, 8)))
    w_up = centred(key_list[6], (SECTIONS, N_EXPERT, D, HID_DEV), D ** -0.5, 0.125, ((0, 4), (1, 8)))
    w_down = centred(key_list[7], (SECTIONS, N_EXPERT, HID_DEV, D), FF ** -0.5, 0.0625, ((0, 4), (1, 8)))
    return {"held": held, "fresh": fresh, "routes": routes, "norm_gain": norm_gain, "router": router, "w_gate": w_gate, "w_up": w_up, "w_down": w_down}


def rms_normed(values, gain):
    mean_square = lax.optimization_barrier(jnp.mean(values * values, axis=-1, keepdims=True))
    return (values * lax.rsqrt(mean_square + 1e-05) * gain).astype(jnp.bfloat16)

def reference(held, fresh, routes, norm_gain, router, w_gate, w_up, w_down):
    rows_cap = N_EXPERT * CAP
    outputs = []
    for section_number in range(SECTIONS):
        if section_number == 0:
            inputs = fresh
        else:
            inputs = held[section_number - 1]
        values = inputs.astype(jnp.float32)
        normed = rms_normed(values, norm_gain[section_number])
        logits = jnp.dot(normed, router[section_number], preferred_element_type=jnp.float32)
        chosen = routes[section_number].astype(jnp.int32)
        picked_logits = jnp.take_along_axis(logits, chosen, axis=1)
        shares = jnp.stack([jax.nn.sigmoid(picked_logits[:, 0] - picked_logits[:, 1]), jax.nn.sigmoid(picked_logits[:, 1] - picked_logits[:, 0])], axis=1)
        gate_all = w_gate[section_number].reshape(EXPERTS, SHARDS, D, HID_DEV)
        up_all = w_up[section_number].reshape(EXPERTS, SHARDS, D, HID_DEV)
        down_all = w_down[section_number].reshape(EXPERTS, SHARDS, HID_DEV, D)
        branch = jnp.zeros((TOKENS, D), jnp.float32)
        for expert_number in range(EXPERTS):
            hits = chosen == expert_number
            weight_share = lax.optimization_barrier(jnp.sum(jnp.where(hits, shares, jnp.zeros_like(shares)), axis=1))
            routed_mask = jnp.any(hits, axis=1)
            token_index = jnp.nonzero(routed_mask, size=rows_cap, fill_value=0)[0].astype(jnp.int32)
            routed_count = jnp.sum(routed_mask.astype(jnp.int32))
            live_rows = (jnp.arange(rows_cap, dtype=jnp.int32) < routed_count).astype(jnp.float32)
            picked_rows = normed[token_index]
            gate_matrix = jnp.transpose(gate_all[expert_number], (1, 0, 2)).reshape(D, FF)
            up_matrix = jnp.transpose(up_all[expert_number], (1, 0, 2)).reshape(D, FF)
            gate_proj = jnp.dot(picked_rows, gate_matrix, preferred_element_type=jnp.float32)
            up_proj = jnp.dot(picked_rows, up_matrix, preferred_element_type=jnp.float32)
            hidden = (jax.nn.silu(gate_proj) * up_proj).astype(jnp.bfloat16)
            partials = jnp.einsum('rsh,shd->srd', hidden.reshape(rows_cap, SHARDS, HID_DEV).astype(jnp.float32), down_all[expert_number].astype(jnp.float32)).astype(jnp.bfloat16)
            expert_out = lax.optimization_barrier(jnp.sum(partials.astype(jnp.float32), axis=0)).astype(jnp.bfloat16)
            expert_out = lax.optimization_barrier(expert_out).astype(jnp.float32)
            scaled = (weight_share[token_index] * live_rows)[:, None] * expert_out
            branch = branch.at[token_index].add(scaled)
        outputs.append((values + branch).astype(jnp.bfloat16))
    return jnp.stack(outputs)
```

```python
import functools

import jax
import jax.numpy as jnp
from jax import lax
from jax.experimental import pallas as pl
from jax.experimental.pallas import tpu as pltpu
from jax.sharding import PartitionSpec as P

MIB = 2**20
VMEM = pl.BlockSpec(memory_space=pltpu.VMEM)
HBM = pl.BlockSpec(memory_space=pltpu.HBM)


def passed_along(x, axis, by):
    length = lax.axis_size(axis)
    pairs = [(i, i + by) for i in range(length) if 0 <= i + by < length]
    return lax.ppermute(x, axis, pairs)


def swapped(x, k):
    length = lax.axis_size("expert")
    return lax.ppermute(x, "expert", [(i, i ^ k) for i in range(length)])


def slot_hits(routes, experts, capacity, route):
    tokens = routes.shape[1]
    me = lax.axis_index("expert")
    ids = lax.broadcasted_iota(jnp.int32, (experts, tokens), 0) ^ me
    first = (routes[0:1] == ids).astype(jnp.float32)
    second = (routes[1:2] == ids).astype(jnp.float32)
    hits = first + second
    before = lax.broadcasted_iota(jnp.int32, (tokens, tokens), 0) < lax.broadcasted_iota(
        jnp.int32, (tokens, tokens), 1
    )
    rank = jnp.dot(hits, before.astype(jnp.float32), preferred_element_type=jnp.float32)
    slots = lax.broadcasted_iota(jnp.int32, (experts, capacity, tokens), 1).astype(jnp.float32)
    chosen = {0: first, 1: second, None: hits}[route]
    placed = jnp.where(slots == rank[:, None, :], chosen[:, None, :], 0.0)
    return placed.reshape(experts * capacity, tokens)


def normed_rows(values, gain):
    mean_square = jnp.mean(values * values, axis=-1, keepdims=True)
    return (values * lax.rsqrt(mean_square + 1e-05) * gain).astype(jnp.bfloat16)


def prepare_kernel(
    experts, capacity, fresh, routes, gain, placing, fresh_here, routes_here, gain_here, sems
):
    pairs = ((routes, routes_here), (fresh, fresh_here), (gain, gain_here))
    copies = [pltpu.make_async_copy(a, b, sems.at[i]) for i, (a, b) in enumerate(pairs)]
    for copy in copies:
        copy.start()
    copies[0].wait()
    placing[...] = slot_hits(routes_here[...], experts, capacity, None).astype(jnp.bfloat16)
    copies[1].wait()
    copies[2].wait()


def pack_kernel(received, fresh, gain, placing, inputs, normed, *blocks):
    section = lax.axis_index("pipe")
    tile = jnp.where(section == 0, fresh[...], received[...])
    inputs[...] = tile
    rows = normed_rows(tile.astype(jnp.float32), gain[...])
    normed[...] = rows
    capacity = blocks[0].shape[0]
    packed = jnp.dot(placing[...], rows, preferred_element_type=jnp.float32).astype(jnp.bfloat16)
    for k, block in enumerate(blocks):
        block[...] = packed[k * capacity : (k + 1) * capacity]


def weigh_kernel(normed, router, routes, weights):
    experts = router.shape[0]
    capacity = weights.shape[1] // experts
    logits = lax.dot_general(
        router[...], normed[...], (((1,), (1,)), ((), ())), preferred_element_type=jnp.float32
    )
    tokens = logits.shape[1]
    ids = lax.broadcasted_iota(jnp.int32, (experts, tokens), 0)
    picked = [
        jnp.sum(jnp.where(routes[r : r + 1, :] == ids, logits, 0.0), axis=0, keepdims=True)
        for r in range(2)
    ]
    total = 0.0
    for r in range(2):
        share = jax.nn.sigmoid(picked[r] - picked[1 - r])
        total += slot_hits(routes[...], experts, capacity, r) * share
    for term in range(3):
        part = total.astype(jnp.bfloat16)
        weights[term] = part
        total = total - part.astype(jnp.float32)


def ffn_kernel(chunk, ring, *refs):
    count = (len(refs) - 7) // 2
    blocks, (gate, up, down), outs = refs[:count], refs[count : count + 3], refs[count + 3 : 2 * count + 3]
    rows, total, slots, sems = refs[2 * count + 3 :][:4]
    capacity = blocks[0].shape[0]
    piece = slots.shape[1]
    per_chunk = chunk // piece
    pieces = down.shape[0] // piece

    def fetch(i):
        return pltpu.make_async_copy(
            down.at[pl.ds(i * piece, piece)], slots.at[lax.rem(i, ring)], sems.at[lax.rem(i, ring)]
        )

    for i in range(ring):
        fetch(i).start()
    for k in range(count):
        rows[k * capacity : (k + 1) * capacity, :] = blocks[k][...]
    total[...] = jnp.zeros_like(total)

    def step(c, _):
        columns = pl.ds(pl.multiple_of(c * chunk, chunk), chunk)
        x = rows[...]
        gate_proj = jnp.dot(x, gate[:, columns], preferred_element_type=jnp.float32)
        up_proj = jnp.dot(x, up[:, columns], preferred_element_type=jnp.float32)
        hidden = (jax.nn.silu(gate_proj) * up_proj).astype(jnp.bfloat16)
        for j in range(per_chunk):
            i = c * per_chunk + j
            fetch(i).wait()
        parts = [
            jnp.dot(
                hidden[:, j * piece : (j + 1) * piece],
                slots[lax.rem(c * per_chunk + j, ring)],
                preferred_element_type=jnp.float32,
            )
            for j in range(per_chunk)
        ]
        total[...] += functools.reduce(lambda a, b: a + b, parts)
        for j in range(per_chunk):
            i = c * per_chunk + j

            @pl.when(i + ring < pieces)
            def _():
                fetch(i + ring).start()

        return 0

    lax.fori_loop(0, down.shape[0] // chunk, step, 0)
    for k in range(count):
        outs[k][...] = total[k * capacity : (k + 1) * capacity, :].astype(jnp.bfloat16)


def combine_kernel(order, inputs, weights, *refs):
    blocks, out, back = refs[:-2], refs[-2], refs[-1]
    capacity = blocks[0].shape[0]
    for k, block in zip(order, blocks):
        back[k * capacity : (k + 1) * capacity, :] = block[...]
    branch = 0.0
    for term in range(3):
        branch += lax.dot_general(
            weights[term], back[...], (((0,), (0,)), ((), ())), preferred_element_type=jnp.float32
        )
    out[...] = (inputs[...].astype(jnp.float32) + branch).astype(jnp.bfloat16)


def in_vmem(x):
    return pltpu.with_memory_space_constraint(x, pltpu.VMEM)


def in_hbm(x):
    return pltpu.with_memory_space_constraint(x, pltpu.HBM)


def call(kernel, out_shape, in_specs, flops=0, moved=0, limit=2 * MIB, scratch=()):
    return pl.pallas_call(
        kernel,
        out_shape=out_shape,
        in_specs=in_specs,
        out_specs=jax.tree.map(lambda _: VMEM, out_shape),
        scratch_shapes=scratch,
        compiler_params=pltpu.CompilerParams(vmem_limit_bytes=limit),
        cost_estimate=pl.CostEstimate(flops=flops, bytes_accessed=moved, transcendentals=0),
    )


def one_expert_each(held, fresh, routes, norm_gain, router, w_gate, w_up, w_down):
    tokens, width = fresh.shape
    experts = router.shape[2]
    capacity = tokens // 2
    slots = experts * capacity
    hidden_units = w_gate.shape[3]
    bf16 = jnp.bfloat16
    chosen = jnp.transpose(routes[0])
    router_rows = jnp.transpose(router[0])
    received = passed_along(held[0], "pipe", 1)
    placing, fresh_here, routes_here, gain_here = call(
        functools.partial(prepare_kernel, experts, capacity),
        [
            pltpu.VMEM((slots, tokens), bf16),
            pltpu.VMEM(fresh.shape, bf16),
            pltpu.VMEM(chosen.shape, jnp.int32),
            pltpu.VMEM(norm_gain.shape, jnp.float32),
        ],
        [HBM] * 3,
        flops=10**6,
        moved=10**6,
        scratch=[pltpu.SemaphoreType.DMA((3,))],
    )(*map(in_hbm, (fresh, chosen, norm_gain)))
    tile = pltpu.VMEM((tokens, width), bf16)
    block = pltpu.VMEM((capacity, width), bf16)
    inputs, normed, *packed = call(
        pack_kernel, [tile, tile] + [block] * experts, [VMEM] * 4, flops=30 * 10**9, moved=10**6
    )(*map(in_vmem, (received, fresh_here, gain_here, placing)))
    order = range(experts - 1, -1, -1)
    arrived = [swapped(packed[k], k) if k else packed[k] for k in order]
    weights = call(
        weigh_kernel, pltpu.VMEM((3, slots, tokens), bf16), [VMEM] * 3, flops=10**6, moved=10**5
    )(in_vmem(normed), router_rows, in_vmem(routes_here))
    weights_in = [in_vmem(w_gate[0, 0]), in_vmem(w_up[0, 0]), in_hbm(w_down[0, 0])]
    piece, ring, chunk = 256, 3, 512
    results = call(
        functools.partial(ffn_kernel, chunk, ring),
        [block] * experts,
        [VMEM] * (experts + 2) + [HBM],
        flops=6 * slots * width * hidden_units,
        moved=6 * width * hidden_units,
        limit=6 * MIB,
        scratch=[
            pltpu.VMEM((slots, width), bf16),
            pltpu.VMEM((slots, width), jnp.float32),
            pltpu.VMEM((ring, piece, width), bf16),
            pltpu.SemaphoreType.DMA((ring,)),
        ],
    )(*map(in_vmem, arrived), *weights_in)
    returned = [swapped(result, k) if k else result for result, k in zip(results, order)]
    out = call(
        functools.partial(combine_kernel, order),
        jax.ShapeDtypeStruct((tokens, width), bf16),
        [VMEM] * (experts + 2),
        flops=10**8,
        moved=10**6,
        limit=4 * MIB,
        scratch=[pltpu.VMEM((slots, width), bf16)],
    )(*map(in_vmem, (inputs, weights, *returned)))
    return out[None]


def shared_experts(held, fresh, routes, norm_gain, router, w_gate, w_up, w_down):
    tok_rows = fresh.shape[0]
    model_width = fresh.shape[1]
    experts = router.shape[2]
    devices = lax.axis_size("expert")
    shard_count = devices // experts
    capacity = tok_rows // 2
    received = passed_along(held[0], "pipe", 1)
    section_index = lax.axis_index("pipe")
    inputs = jnp.where(section_index == 0, fresh, received)
    values = inputs.astype(jnp.float32)
    normed = normed_rows(values, norm_gain[0])
    logits = jnp.dot(normed, router[0], preferred_element_type=jnp.float32)
    chosen = routes[0]
    expert_ids = jnp.arange(experts, dtype=jnp.int32)
    token_hits = (chosen[:, :, None] == expert_ids[None, None, :]).astype(jnp.float32)
    picked_logits = jnp.sum(token_hits * logits[:, None, :], axis=2)
    shares = jnp.stack(
        [
            jax.nn.sigmoid(picked_logits[:, 0] - picked_logits[:, 1]),
            jax.nn.sigmoid(picked_logits[:, 1] - picked_logits[:, 0]),
        ],
        axis=1,
    )
    flat_choice = chosen.reshape(-1)
    onehot = (flat_choice[:, None] == expert_ids[None, :]).astype(jnp.int32)
    rank_table = jnp.cumsum(onehot, axis=0) - 1
    slot_index = jnp.sum(onehot * rank_table, axis=1)
    target = flat_choice * capacity + slot_index
    slot_ids = jnp.arange(experts * capacity, dtype=jnp.int32)
    placing = (target[:, None] == slot_ids[None, :]).astype(jnp.bfloat16)
    placing_tok = jnp.sum(placing.reshape(tok_rows, 2, experts * capacity), axis=1)
    buffer = jnp.dot(placing_tok.T, normed, preferred_element_type=jnp.float32).astype(jnp.bfloat16)
    gate_matrix = w_gate[0, 0]
    up_matrix = w_up[0, 0]
    down_matrix = w_down[0, 0]
    outgoing = jnp.broadcast_to(
        buffer.reshape(experts, 1, capacity, model_width),
        (experts, shard_count, capacity, model_width),
    )
    outgoing = outgoing.reshape(devices, capacity, model_width)
    row_block = lax.all_to_all(outgoing, "expert", split_axis=0, concat_axis=0, tiled=True)
    flat_rows = row_block.reshape(-1, model_width)
    gate_proj = jnp.dot(flat_rows, gate_matrix, preferred_element_type=jnp.float32)
    up_proj = jnp.dot(flat_rows, up_matrix, preferred_element_type=jnp.float32)
    hidden = (jax.nn.silu(gate_proj) * up_proj).astype(jnp.bfloat16)
    partial_value = jnp.dot(hidden, down_matrix, preferred_element_type=jnp.float32).astype(
        jnp.bfloat16
    )
    came_back = lax.all_to_all(
        partial_value.reshape(row_block.shape), "expert", split_axis=0, concat_axis=0, tiled=True
    )
    expert_out = jnp.sum(
        came_back.reshape(experts, shard_count, capacity, model_width).astype(jnp.float32), axis=1
    ).astype(jnp.bfloat16)
    picked = jnp.dot(
        placing,
        expert_out.reshape(experts * capacity, model_width),
        preferred_element_type=jnp.float32,
    )
    picked = picked.reshape(tok_rows, 2, model_width)
    branch = shares[:, 0, None] * picked[:, 0] + shares[:, 1, None] * picked[:, 1]
    section_out = (values + branch).astype(jnp.bfloat16)
    return section_out[None]


def per_device(*args):
    experts = args[4].shape[2]
    alone = lax.axis_size("expert") == experts and experts & (experts - 1) == 0
    return (one_expert_each if alone else shared_experts)(*args)


def solution(mesh):
    in_specs = (
        P("pipe", "expert", None),
        P("expert", None),
        P("pipe", "expert", None),
        P("pipe", None),
        P("pipe", None, None),
        P("pipe", "expert", None, None),
        P("pipe", "expert", None, None),
        P("pipe", "expert", None, None),
    )
    out_specs = P("pipe", "expert", None)
    return jax.shard_map(
        per_device, mesh=mesh, in_specs=in_specs, out_specs=out_specs, check_vma=False
    )
```

```python
import functools

import jax
import jax.numpy as jnp
from jax import lax
from jax.experimental import pallas as pl
from jax.experimental.pallas import tpu as pltpu
from jax.sharding import PartitionSpec as P

MIB = 2**20
CHUNK, BAND = 1024, 512
HEAD = 4096
TERMS = 3
VMEM = pl.BlockSpec(memory_space=pltpu.VMEM)
HBM = pl.BlockSpec(memory_space=pltpu.HBM)


def passed_along(x, axis, by):
    length = lax.axis_size(axis)
    pairs = [(i, i + by) for i in range(length) if 0 <= i + by < length]
    return lax.ppermute(x, axis, pairs)


def swapped(x, k):
    length = lax.axis_size("expert")
    return lax.ppermute(x, "expert", [(i, i ^ k) for i in range(length)])


def slot_hits(routes, experts, capacity, route):
    tokens = routes.shape[1]
    me = lax.axis_index("expert")
    ids = lax.broadcasted_iota(jnp.int32, (experts, tokens), 0) ^ me
    first = (routes[0:1] == ids).astype(jnp.float32)
    second = (routes[1:2] == ids).astype(jnp.float32)
    hits = first + second
    before = lax.broadcasted_iota(jnp.int32, (tokens, tokens), 0) < lax.broadcasted_iota(
        jnp.int32, (tokens, tokens), 1
    )
    rank = jnp.dot(hits, before.astype(jnp.float32), preferred_element_type=jnp.float32)
    slots = lax.broadcasted_iota(jnp.int32, (experts, capacity, tokens), 1).astype(jnp.float32)
    chosen = {0: first, 1: second, None: hits}[route]
    placed = jnp.where(slots == rank[:, None, :], chosen[:, None, :], 0.0)
    return placed.reshape(experts * capacity, tokens)


def normed_rows(values, gain):
    mean_square = jnp.mean(values * values, axis=-1, keepdims=True)
    return (values * lax.rsqrt(mean_square + 1e-05) * gain).astype(jnp.bfloat16)


def prepare_kernel(
    experts, capacity, fresh, routes, gain, placing, fresh_here, routes_here, gain_here, sems
):
    pairs = ((routes, routes_here), (fresh, fresh_here), (gain, gain_here))
    copies = [pltpu.make_async_copy(a, b, sems.at[i]) for i, (a, b) in enumerate(pairs)]
    for copy in copies:
        copy.start()
    copies[0].wait()
    placing[...] = slot_hits(routes_here[...], experts, capacity, None).astype(jnp.bfloat16)
    for copy in copies[1:]:
        copy.wait()


def pack_kernel(received, fresh, gain, placing, inputs, normed, *blocks):
    section = lax.axis_index("pipe")
    tile = jnp.where(section == 0, fresh[...], received[...])
    inputs[...] = tile
    rows = normed_rows(tile.astype(jnp.float32), gain[...])
    normed[...] = rows
    capacity = blocks[0].shape[0]
    packed = jnp.dot(placing[...], rows, preferred_element_type=jnp.float32).astype(jnp.bfloat16)
    for k, block in enumerate(blocks):
        block[...] = packed[k * capacity : (k + 1) * capacity]


def weigh_kernel(head, normed, router, routes, up, weights, up_here, sem):
    fetch = pltpu.make_async_copy(up.at[:, :head], up_here.at[:, :head], sem)
    fetch.start()
    experts = router.shape[0]
    slots = weights.shape[1]
    logits = lax.dot_general(
        router[...], normed[...], (((1,), (1,)), ((), ())), preferred_element_type=jnp.float32
    )
    tokens = logits.shape[1]
    ids = lax.broadcasted_iota(jnp.int32, (experts, tokens), 0)
    picked = [
        jnp.sum(jnp.where(routes[r : r + 1, :] == ids, logits, 0.0), axis=0, keepdims=True)
        for r in range(2)
    ]
    total = 0.0
    for r in range(2):
        share = jax.nn.sigmoid(picked[r] - picked[1 - r])
        total += slot_hits(routes[...], experts, slots // experts, r) * share
    diagonal = lax.broadcasted_iota(jnp.int32, (slots, slots), 0) == lax.broadcasted_iota(
        jnp.int32, (slots, slots), 1
    )
    for term in range(TERMS):
        part = total.astype(jnp.bfloat16)
        weights[term * tokens : (term + 1) * tokens, :] = lax.dot_general(
            part,
            diagonal.astype(jnp.bfloat16),
            (((0,), (0,)), ((), ())),
            preferred_element_type=jnp.float32,
        ).astype(jnp.bfloat16)
        total = total - part.astype(jnp.float32)
    fetch.wait()


def ffn_kernel(count, chunk, band, head, *refs):
    blocks, (gate, _, up, down) = refs[:count], refs[count : count + 4]
    outs = refs[count + 4 : 2 * count + 4]
    spare, rows, hidden, sems, tail_sems = refs[2 * count + 4 :]
    capacity = blocks[0].shape[0]
    width, hidden_units = gate.shape
    unit = width // 2
    tall = hidden_units // unit

    def place(u):
        return pl.ds(u % 2 * unit, unit), pl.ds(u // 2 * band, band)

    def fetch(u):
        source = down.at[pl.ds(u % tall * unit, unit), pl.ds(u // tall * band, band)]
        return pltpu.make_async_copy(source, spare.at[place(u)], sems.at[u])

    def fetch_tail(c):
        columns = pl.ds(pl.multiple_of(c * chunk, chunk), chunk)
        return pltpu.make_async_copy(up.at[:, columns], spare.at[:, columns], tail_sems.at[c - head // chunk])

    for c in range(head // chunk, hidden_units // chunk):
        fetch_tail(c).start()
    for k in range(count):
        rows[k * capacity : (k + 1) * capacity, :] = blocks[k][...]

    def step(c, fetched):
        columns = pl.ds(pl.multiple_of(c * chunk, chunk), chunk)
        x = rows[...]
        if not fetched:
            fetch_tail(c).wait()
        gate_proj = jnp.dot(x, gate[:, columns], preferred_element_type=jnp.float32)

        up_proj = jnp.dot(x, spare[:, columns], preferred_element_type=jnp.float32)
        hidden[:, columns] = (jax.nn.silu(gate_proj) * up_proj).astype(jnp.bfloat16)
        for j in range(2 * chunk // band):
            fetch(c * (2 * chunk // band) + j).start()

    pl.loop(0, head // chunk)(lambda c: step(c, True))
    pl.loop(head // chunk, hidden_units // chunk)(lambda c: step(c, False))
    for j in range(width // band):
        total, u = None, j * tall
        while u < (j + 1) * tall:
            paired = u % 2 == 0 and u + 1 < (j + 1) * tall
            for v in range(u, u + 1 + paired):
                fetch(v).wait()
            start, columns = u % 2 * unit, place(u)[1]
            part = jnp.dot(
                hidden[:, u % tall * unit : (u % tall + 1 + paired) * unit],
                spare[start : start + (1 + paired) * unit, columns],
                preferred_element_type=jnp.float32,
            )
            total = part if total is None else total + part
            u += 1 + paired
        for k in range(count):
            outs[k][:, j * band : (j + 1) * band] = total[k * capacity : (k + 1) * capacity].astype(
                jnp.bfloat16
            )


def combine_kernel(order, inputs, weights, *refs):
    blocks, out, back = refs[:-2], refs[-2], refs[-1]
    capacity = blocks[0].shape[0]
    for k, block in zip(order, blocks):
        back[k * capacity : (k + 1) * capacity, :] = block[...]
    terms = jnp.dot(weights[...], back[...], preferred_element_type=jnp.float32)
    total = inputs[...].astype(jnp.float32)
    tokens = total.shape[0]
    for term in range(TERMS):
        total += terms[term * tokens : (term + 1) * tokens]
    out[...] = total.astype(jnp.bfloat16)


def in_vmem(x):
    return pltpu.with_memory_space_constraint(x, pltpu.VMEM)


def in_hbm(x):
    return pltpu.with_memory_space_constraint(x, pltpu.HBM)


def call(kernel, out_shape, in_specs, flops=0, moved=0, limit=2 * MIB, scratch=(), aliases={}):
    return pl.pallas_call(
        kernel,
        out_shape=out_shape,
        in_specs=in_specs,
        out_specs=jax.tree.map(lambda _: VMEM, out_shape),
        scratch_shapes=scratch,
        input_output_aliases=aliases,
        compiler_params=pltpu.CompilerParams(vmem_limit_bytes=limit),
        cost_estimate=pl.CostEstimate(flops=flops, bytes_accessed=moved, transcendentals=0),
    )


def one_expert_each(held, fresh, routes, norm_gain, router, w_gate, w_up, w_down):
    tokens, width = fresh.shape
    experts = router.shape[2]
    capacity = tokens // 2
    slots = experts * capacity
    hidden_units = w_gate.shape[3]
    bf16 = jnp.bfloat16
    chosen = jnp.transpose(routes[0])
    router_rows = jnp.transpose(router[0])
    received = passed_along(held[0], "pipe", 1)
    placing, fresh_here, routes_here, gain_here = call(
        functools.partial(prepare_kernel, experts, capacity),
        [
            pltpu.VMEM((slots, tokens), bf16),
            pltpu.VMEM(fresh.shape, bf16),
            pltpu.VMEM(chosen.shape, jnp.int32),
            pltpu.VMEM(norm_gain.shape, jnp.float32),
        ],
        [HBM] * 3,
        flops=60 * 10**9,
        moved=10**6,
        scratch=[pltpu.SemaphoreType.DMA((3,))],
    )(*map(in_hbm, (fresh, chosen, norm_gain)))
    tile = pltpu.VMEM((tokens, width), bf16)
    block = pltpu.VMEM((capacity, width), bf16)
    inputs, normed, *packed = call(
        pack_kernel, [tile, tile] + [block] * experts, [VMEM] * 4, flops=10**7, moved=10**6
    )(*map(in_vmem, (received, fresh_here, gain_here, placing)))
    order = range(experts - 1, -1, -1)
    arrived = [swapped(packed[k], k) if k else packed[k] for k in order]
    head = min(HEAD, hidden_units)
    weights, up_here = call(
        functools.partial(weigh_kernel, head),
        [pltpu.VMEM((TERMS * tokens, slots), bf16), pltpu.VMEM((width, hidden_units), bf16)],
        [VMEM] * 3 + [HBM],
        flops=10**6,
        moved=2 * width * head,
        scratch=[pltpu.SemaphoreType.DMA],
    )(in_vmem(normed), router_rows, in_vmem(routes_here), in_hbm(w_up[0, 0]))
    *results, _ = call(
        functools.partial(ffn_kernel, experts, CHUNK, BAND, head),
        [block] * experts + [pltpu.VMEM((width, hidden_units), bf16)],
        [VMEM] * (experts + 2) + [HBM, HBM],
        flops=6 * slots * width * hidden_units,
        moved=6 * width * hidden_units,
        limit=6 * MIB,
        scratch=[
            pltpu.VMEM((slots, width), bf16),
            pltpu.VMEM((slots, hidden_units), bf16),
            pltpu.SemaphoreType.DMA((2 * hidden_units // BAND,)),
            pltpu.SemaphoreType.DMA((max(1, (hidden_units - head) // CHUNK),)),
        ],
        aliases={experts + 1: experts},
    )(*map(in_vmem, arrived), in_vmem(w_gate[0, 0]), in_vmem(up_here), in_hbm(w_up[0, 0]), in_hbm(w_down[0, 0]))
    returned = [swapped(result, k) if k else result for result, k in zip(results, order)]
    out = call(
        functools.partial(combine_kernel, order),
        jax.ShapeDtypeStruct((tokens, width), bf16),
        [VMEM] * (experts + 2),
        flops=10**8,
        moved=10**6,
        limit=4 * MIB,
        scratch=[pltpu.VMEM((slots, width), bf16)],
    )(*map(in_vmem, (inputs, weights, *returned)))
    return out[None]


def shared_experts(held, fresh, routes, norm_gain, router, w_gate, w_up, w_down):
    tok_rows = fresh.shape[0]
    model_width = fresh.shape[1]
    experts = router.shape[2]
    devices = lax.axis_size("expert")
    shard_count = devices // experts
    capacity = tok_rows // 2
    received = passed_along(held[0], "pipe", 1)
    section_index = lax.axis_index("pipe")
    inputs = jnp.where(section_index == 0, fresh, received)
    values = inputs.astype(jnp.float32)
    normed = normed_rows(values, norm_gain[0])
    logits = jnp.dot(normed, router[0], preferred_element_type=jnp.float32)
    chosen = routes[0]
    expert_ids = jnp.arange(experts, dtype=jnp.int32)
    token_hits = (chosen[:, :, None] == expert_ids[None, None, :]).astype(jnp.float32)
    picked_logits = jnp.sum(token_hits * logits[:, None, :], axis=2)
    shares = jnp.stack(
        [
            jax.nn.sigmoid(picked_logits[:, 0] - picked_logits[:, 1]),
            jax.nn.sigmoid(picked_logits[:, 1] - picked_logits[:, 0]),
        ],
        axis=1,
    )
    flat_choice = chosen.reshape(-1)
    onehot = (flat_choice[:, None] == expert_ids[None, :]).astype(jnp.int32)
    rank_table = jnp.cumsum(onehot, axis=0) - 1
    slot_index = jnp.sum(onehot * rank_table, axis=1)
    target = flat_choice * capacity + slot_index
    slot_ids = jnp.arange(experts * capacity, dtype=jnp.int32)
    placing = (target[:, None] == slot_ids[None, :]).astype(jnp.bfloat16)
    placing_tok = jnp.sum(placing.reshape(tok_rows, 2, experts * capacity), axis=1)
    buffer = jnp.dot(placing_tok.T, normed, preferred_element_type=jnp.float32).astype(jnp.bfloat16)
    gate_matrix = w_gate[0, 0]
    up_matrix = w_up[0, 0]
    down_matrix = w_down[0, 0]
    outgoing = jnp.broadcast_to(
        buffer.reshape(experts, 1, capacity, model_width),
        (experts, shard_count, capacity, model_width),
    )
    outgoing = outgoing.reshape(devices, capacity, model_width)
    row_block = lax.all_to_all(outgoing, "expert", split_axis=0, concat_axis=0, tiled=True)
    flat_rows = row_block.reshape(-1, model_width)
    gate_proj = jnp.dot(flat_rows, gate_matrix, preferred_element_type=jnp.float32)
    up_proj = jnp.dot(flat_rows, up_matrix, preferred_element_type=jnp.float32)
    hidden = (jax.nn.silu(gate_proj) * up_proj).astype(jnp.bfloat16)
    partial_value = jnp.dot(hidden, down_matrix, preferred_element_type=jnp.float32).astype(
        jnp.bfloat16
    )
    came_back = lax.all_to_all(
        partial_value.reshape(row_block.shape), "expert", split_axis=0, concat_axis=0, tiled=True
    )
    expert_out = jnp.sum(
        came_back.reshape(experts, shard_count, capacity, model_width).astype(jnp.float32), axis=1
    ).astype(jnp.bfloat16)
    picked = jnp.dot(
        placing,
        expert_out.reshape(experts * capacity, model_width),
        preferred_element_type=jnp.float32,
    )
    picked = picked.reshape(tok_rows, 2, model_width)
    branch = shares[:, 0, None] * picked[:, 0] + shares[:, 1, None] * picked[:, 1]
    section_out = (values + branch).astype(jnp.bfloat16)
    return section_out[None]


def per_device(*args):
    experts = args[4].shape[2]
    width, hidden_units = args[5].shape[2:]
    alone = lax.axis_size("expert") == experts and experts & (experts - 1) == 0
    alone &= hidden_units % CHUNK == 0 and hidden_units % (width // 2) == 0 and width % (2 * BAND) == 0
    return (one_expert_each if alone else shared_experts)(*args)


def solution(mesh):
    in_specs = (
        P("pipe", "expert", None),
        P("expert", None),
        P("pipe", "expert", None),
        P("pipe", None),
        P("pipe", None, None),
        P("pipe", "expert", None, None),
        P("pipe", "expert", None, None),
        P("pipe", "expert", None, None),
    )
    out_specs = P("pipe", "expert", None)
    return jax.shard_map(
        per_device, mesh=mesh, in_specs=in_specs, out_specs=out_specs, check_vma=False
    )
```

```python
import functools

import jax
import jax.numpy as jnp
from jax import lax
from jax.experimental import pallas as pl
from jax.experimental.pallas import tpu as pltpu
from jax.sharding import PartitionSpec as P

MIB = 2**20
CHUNK, BAND = 1024, 512
HEAD = 4096
TERMS = 3
VMEM = pl.BlockSpec(memory_space=pltpu.VMEM)
HBM = pl.BlockSpec(memory_space=pltpu.HBM)


def passed_along(x, axis, by):
    length = lax.axis_size(axis)
    pairs = [(i, i + by) for i in range(length) if 0 <= i + by < length]
    return lax.ppermute(x, axis, pairs)


def swapped(x, k):
    length = lax.axis_size("expert")
    return lax.ppermute(x, "expert", [(i, i ^ k) for i in range(length)])


def slot_hits(routes, experts, capacity, route):
    tokens = routes.shape[1]
    me = lax.axis_index("expert")
    ids = lax.broadcasted_iota(jnp.int32, (experts, tokens), 0) ^ me
    first = (routes[0:1] == ids).astype(jnp.float32)
    second = (routes[1:2] == ids).astype(jnp.float32)
    hits = first + second
    before = lax.broadcasted_iota(jnp.int32, (tokens, tokens), 0) < lax.broadcasted_iota(
        jnp.int32, (tokens, tokens), 1
    )
    rank = jnp.dot(hits, before.astype(jnp.float32), preferred_element_type=jnp.float32)
    slots = lax.broadcasted_iota(jnp.int32, (experts, capacity, tokens), 1).astype(jnp.float32)
    chosen = {0: first, 1: second, None: hits}[route]
    placed = jnp.where(slots == rank[:, None, :], chosen[:, None, :], 0.0)
    return placed.reshape(experts * capacity, tokens)


def normed_rows(values, gain):
    mean_square = jnp.mean(values * values, axis=-1, keepdims=True)
    return (values * lax.rsqrt(mean_square + 1e-05) * gain).astype(jnp.bfloat16)


def tile_comes_late():
    section = lax.axis_index("pipe")
    return (section > 0) & (section < lax.axis_size("pipe") - 1)


def prepare_kernel(
    experts, capacity, fresh, routes, gain, up, placing, fresh_here, routes_here, gain_here, first, sems
):
    pairs = ((routes, routes_here), (fresh, fresh_here), (gain, gain_here))
    copies = [pltpu.make_async_copy(a, b, sems.at[i]) for i, (a, b) in enumerate(pairs)]
    for copy in copies:
        copy.start()

    @pl.when(tile_comes_late())
    def _():
        fetch = pltpu.make_async_copy(up.at[:, : first.shape[1]], first, sems.at[len(pairs)])
        fetch.start()
        fetch.wait()

    copies[0].wait()
    placing[...] = slot_hits(routes_here[...], experts, capacity, None).astype(jnp.bfloat16)
    for copy in copies[1:]:
        copy.wait()


def pack_kernel(received, fresh, gain, placing, inputs, normed, *blocks):
    section = lax.axis_index("pipe")
    tile = jnp.where(section == 0, fresh[...], received[...])
    inputs[...] = tile
    rows = normed_rows(tile.astype(jnp.float32), gain[...])
    normed[...] = rows
    capacity = blocks[0].shape[0]
    packed = jnp.dot(placing[...], rows, preferred_element_type=jnp.float32).astype(jnp.bfloat16)
    for k, block in enumerate(blocks):
        block[...] = packed[k * capacity : (k + 1) * capacity]


def weigh_kernel(first, head, normed, router, routes, up, weights, rest, sems):
    chunk = first
    fetch = pltpu.make_async_copy(up.at[:, chunk:head], rest.at[:, : head - chunk], sems.at[0])
    fetch.start()
    more = pltpu.make_async_copy(
        up.at[:, head : head + chunk], rest.at[:, head - chunk : head], sems.at[1]
    )
    pl.when(~tile_comes_late())(more.start)
    experts = router.shape[0]
    slots = weights.shape[1]
    logits = lax.dot_general(
        router[...], normed[...], (((1,), (1,)), ((), ())), preferred_element_type=jnp.float32
    )
    tokens = logits.shape[1]
    ids = lax.broadcasted_iota(jnp.int32, (experts, tokens), 0)
    picked = [
        jnp.sum(jnp.where(routes[r : r + 1, :] == ids, logits, 0.0), axis=0, keepdims=True)
        for r in range(2)
    ]
    total = 0.0
    for r in range(2):
        share = jax.nn.sigmoid(picked[r] - picked[1 - r])
        total += slot_hits(routes[...], experts, slots // experts, r) * share
    diagonal = lax.broadcasted_iota(jnp.int32, (slots, slots), 0) == lax.broadcasted_iota(
        jnp.int32, (slots, slots), 1
    )
    for term in range(TERMS):
        part = total.astype(jnp.bfloat16)
        weights[term * tokens : (term + 1) * tokens, :] = lax.dot_general(
            part,
            diagonal.astype(jnp.bfloat16),
            (((0,), (0,)), ((), ())),
            preferred_element_type=jnp.float32,
        ).astype(jnp.bfloat16)
        total = total - part.astype(jnp.float32)
    fetch.wait()
    pl.when(~tile_comes_late())(more.wait)


def first_chunk(c):
    return isinstance(c, int) and c == 0


def ffn_kernel(count, band, head, *refs):
    blocks, (gate, _, _, up, down) = refs[:count], refs[count : count + 5]
    outs, spares = refs[count + 5 : 2 * count + 5], refs[2 * count + 5 : 2 * count + 7]
    rows, hidden, sems, tail_sems = refs[2 * count + 7 :]
    capacity = blocks[0].shape[0]
    width, hidden_units = gate.shape
    chunk = spares[0].shape[1]
    unit = width // 2
    tall = hidden_units // unit
    per_chunk = 2 * chunk // band
    loaded, chunks = head // chunk, hidden_units // chunk
    order = [*range(1, loaded), *range(loaded + 1, chunks), 0, loaded]

    def place(u, c):
        late = int(not first_chunk(c))
        left = (c - 1) * chunk if late else 0
        columns = pl.ds(pl.multiple_of(left + u % per_chunk // 2 * band, band), band)
        return spares[late].at[pl.ds(u % 2 * unit, unit), columns]

    def fetch(u, c):
        source = down.at[pl.ds(u % tall * unit, unit), pl.ds(pl.multiple_of(u // tall * band, band), band)]
        return pltpu.make_async_copy(source, place(u, c), sems.at[u])

    def columns_of(c):
        return pl.ds(pl.multiple_of(c * chunk, chunk), chunk)

    def part_of(c):
        return spares[0] if first_chunk(c) else spares[1].at[:, columns_of(c - 1)]

    def fetch_tail(c, slot):
        return pltpu.make_async_copy(up.at[:, columns_of(c)], part_of(c), tail_sems.at[slot])

    for c in range(loaded + 1, chunks):
        fetch_tail(c, c - loaded).start()
    pl.when(tile_comes_late())(fetch_tail(loaded, 0).start)
    pl.when(~tile_comes_late())(fetch_tail(0, 0).start)
    for k in range(count):
        rows[k * capacity : (k + 1) * capacity, :] = blocks[k][...]

    def step(c, turn):
        x = rows[...]
        gate_proj = jnp.dot(x, gate[:, columns_of(c)], preferred_element_type=jnp.float32)
        up_proj = jnp.dot(x, part_of(c)[...], preferred_element_type=jnp.float32)
        hidden[:, columns_of(c)] = (jax.nn.silu(gate_proj) * up_proj).astype(jnp.bfloat16)
        for j in range(per_chunk):
            fetch(turn * per_chunk + j, c).start()

    @pl.loop(0, loaded - 1)
    def _(turn):
        step(turn + 1, turn)

    @pl.loop(loaded - 1, chunks - 2)
    def _(turn):
        fetch_tail(turn + 2, turn + 2 - loaded).wait()
        step(turn + 2, turn)

    fetch_tail(0, 0).wait()
    step(0, chunks - 2)
    step(loaded, chunks - 1)
    for j in range(width // band):
        total, u = None, j * tall
        last = j == width // band - 1
        if not last:
            for v in range(u, u + tall):
                fetch(v, order[v // per_chunk]).wait()
        while u < (j + 1) * tall:
            paired = u % 2 == 0 and u + 1 < (j + 1) * tall
            c = order[u // per_chunk]
            for v in range(u, u + 1 + paired) if last else ():
                fetch(v, c).wait()
            top, left = u % 2 * unit, u % per_chunk // 2 * band
            part = jnp.dot(
                hidden[:, u % tall * unit : (u % tall + 1 + paired) * unit],
                part_of(c)[top : top + (1 + paired) * unit, left : left + band],
                preferred_element_type=jnp.float32,
            )
            total = part if total is None else total + part
            u += 1 + paired
        for k in range(count):
            outs[k][:, j * band : (j + 1) * band] = total[k * capacity : (k + 1) * capacity].astype(
                jnp.bfloat16
            )


def combine_kernel(order, inputs, weights, *refs):
    blocks, out, back = refs[:-2], refs[-2], refs[-1]
    capacity = blocks[0].shape[0]
    for k, block in zip(order, blocks):
        back[k * capacity : (k + 1) * capacity, :] = block[...]
    terms = jnp.dot(weights[...], back[...], preferred_element_type=jnp.float32)
    total = inputs[...].astype(jnp.float32)
    tokens = total.shape[0]
    for term in range(TERMS):
        total += terms[term * tokens : (term + 1) * tokens]
    out[...] = total.astype(jnp.bfloat16)


def in_vmem(x):
    return pltpu.with_memory_space_constraint(x, pltpu.VMEM)


def in_hbm(x):
    return pltpu.with_memory_space_constraint(x, pltpu.HBM)


def call(kernel, out_shape, in_specs, flops=0, moved=0, limit=2 * MIB, scratch=(), aliases={}):
    return pl.pallas_call(
        kernel,
        out_shape=out_shape,
        in_specs=in_specs,
        out_specs=jax.tree.map(lambda _: VMEM, out_shape),
        scratch_shapes=scratch,
        input_output_aliases=aliases,
        compiler_params=pltpu.CompilerParams(vmem_limit_bytes=limit),
        cost_estimate=pl.CostEstimate(flops=flops, bytes_accessed=moved, transcendentals=0),
    )


def one_expert_each(held, fresh, routes, norm_gain, router, w_gate, w_up, w_down):
    tokens, width = fresh.shape
    experts = router.shape[2]
    capacity = tokens // 2
    slots = experts * capacity
    hidden_units = w_gate.shape[3]
    bf16 = jnp.bfloat16
    chosen = jnp.transpose(routes[0])
    router_rows = jnp.transpose(router[0])
    received = passed_along(held[0], "pipe", 1)
    placing, fresh_here, routes_here, gain_here, up_first = call(
        functools.partial(prepare_kernel, experts, capacity),
        [
            pltpu.VMEM((slots, tokens), bf16),
            pltpu.VMEM(fresh.shape, bf16),
            pltpu.VMEM(chosen.shape, jnp.int32),
            pltpu.VMEM(norm_gain.shape, jnp.float32),
            pltpu.VMEM((width, CHUNK), bf16),
        ],
        [HBM] * 4,
        flops=60 * 10**9,
        moved=10**6,
        scratch=[pltpu.SemaphoreType.DMA((4,))],
    )(*map(in_hbm, (fresh, chosen, norm_gain, w_up[0, 0])))
    tile = pltpu.VMEM((tokens, width), bf16)
    block = pltpu.VMEM((capacity, width), bf16)
    inputs, normed, *packed = call(
        pack_kernel, [tile, tile] + [block] * experts, [VMEM] * 4, flops=10**7, moved=10**6
    )(*map(in_vmem, (received, fresh_here, gain_here, placing)))
    order = range(experts - 1, -1, -1)
    arrived = [swapped(packed[k], k) if k else packed[k] for k in order]
    weights, up_rest = call(
        functools.partial(weigh_kernel, CHUNK, HEAD),
        [pltpu.VMEM((TERMS * tokens, slots), bf16), pltpu.VMEM((width, hidden_units - CHUNK), bf16)],
        [VMEM] * 3 + [HBM],
        flops=10**6,
        moved=2 * width * HEAD,
        scratch=[pltpu.SemaphoreType.DMA((2,))],
    )(in_vmem(normed), router_rows, in_vmem(routes_here), in_hbm(w_up[0, 0]))
    *results, _, _ = call(
        functools.partial(ffn_kernel, experts, BAND, HEAD),
        [block] * experts + [pltpu.VMEM(up.shape, bf16) for up in (up_first, up_rest)],
        [VMEM] * (experts + 3) + [HBM, HBM],
        flops=6 * slots * width * hidden_units,
        moved=6 * width * hidden_units,
        limit=6 * MIB,
        scratch=[
            pltpu.VMEM((slots, width), bf16),
            pltpu.VMEM((slots, hidden_units), bf16),
            pltpu.SemaphoreType.DMA((2 * hidden_units // BAND,)),
            pltpu.SemaphoreType.DMA(((hidden_units - HEAD) // CHUNK,)),
        ],
        aliases={experts + 1: experts, experts + 2: experts + 1},
    )(*map(in_vmem, arrived), *map(in_vmem, (w_gate[0, 0], up_first, up_rest)), *map(in_hbm, (w_up[0, 0], w_down[0, 0])))
    returned = [swapped(result, k) if k else result for result, k in zip(results, order)]
    out = call(
        functools.partial(combine_kernel, order),
        jax.ShapeDtypeStruct((tokens, width), bf16),
        [VMEM] * (experts + 2),
        flops=10**8,
        moved=10**6,
        limit=4 * MIB,
        scratch=[pltpu.VMEM((slots, width), bf16)],
    )(*map(in_vmem, (inputs, weights, *returned)))
    return out[None]


def shared_experts(held, fresh, routes, norm_gain, router, w_gate, w_up, w_down):
    tok_rows = fresh.shape[0]
    model_width = fresh.shape[1]
    experts = router.shape[2]
    devices = lax.axis_size("expert")
    shard_count = devices // experts
    capacity = tok_rows // 2
    received = passed_along(held[0], "pipe", 1)
    section_index = lax.axis_index("pipe")
    inputs = jnp.where(section_index == 0, fresh, received)
    values = inputs.astype(jnp.float32)
    normed = normed_rows(values, norm_gain[0])
    logits = jnp.dot(normed, router[0], preferred_element_type=jnp.float32)
    chosen = routes[0]
    expert_ids = jnp.arange(experts, dtype=jnp.int32)
    token_hits = (chosen[:, :, None] == expert_ids[None, None, :]).astype(jnp.float32)
    picked_logits = jnp.sum(token_hits * logits[:, None, :], axis=2)
    shares = jnp.stack(
        [
            jax.nn.sigmoid(picked_logits[:, 0] - picked_logits[:, 1]),
            jax.nn.sigmoid(picked_logits[:, 1] - picked_logits[:, 0]),
        ],
        axis=1,
    )
    flat_choice = chosen.reshape(-1)
    onehot = (flat_choice[:, None] == expert_ids[None, :]).astype(jnp.int32)
    rank_table = jnp.cumsum(onehot, axis=0) - 1
    slot_index = jnp.sum(onehot * rank_table, axis=1)
    target = flat_choice * capacity + slot_index
    slot_ids = jnp.arange(experts * capacity, dtype=jnp.int32)
    placing = (target[:, None] == slot_ids[None, :]).astype(jnp.bfloat16)
    placing_tok = jnp.sum(placing.reshape(tok_rows, 2, experts * capacity), axis=1)
    buffer = jnp.dot(placing_tok.T, normed, preferred_element_type=jnp.float32).astype(jnp.bfloat16)
    gate_matrix = w_gate[0, 0]
    up_matrix = w_up[0, 0]
    down_matrix = w_down[0, 0]
    outgoing = jnp.broadcast_to(
        buffer.reshape(experts, 1, capacity, model_width),
        (experts, shard_count, capacity, model_width),
    )
    outgoing = outgoing.reshape(devices, capacity, model_width)
    row_block = lax.all_to_all(outgoing, "expert", split_axis=0, concat_axis=0, tiled=True)
    flat_rows = row_block.reshape(-1, model_width)
    gate_proj = jnp.dot(flat_rows, gate_matrix, preferred_element_type=jnp.float32)
    up_proj = jnp.dot(flat_rows, up_matrix, preferred_element_type=jnp.float32)
    hidden = (jax.nn.silu(gate_proj) * up_proj).astype(jnp.bfloat16)
    partial_value = jnp.dot(hidden, down_matrix, preferred_element_type=jnp.float32).astype(
        jnp.bfloat16
    )
    came_back = lax.all_to_all(
        partial_value.reshape(row_block.shape), "expert", split_axis=0, concat_axis=0, tiled=True
    )
    expert_out = jnp.sum(
        came_back.reshape(experts, shard_count, capacity, model_width).astype(jnp.float32), axis=1
    ).astype(jnp.bfloat16)
    picked = jnp.dot(
        placing,
        expert_out.reshape(experts * capacity, model_width),
        preferred_element_type=jnp.float32,
    )
    picked = picked.reshape(tok_rows, 2, model_width)
    branch = shares[:, 0, None] * picked[:, 0] + shares[:, 1, None] * picked[:, 1]
    section_out = (values + branch).astype(jnp.bfloat16)
    return section_out[None]


def per_device(*args):
    experts = args[4].shape[2]
    width, hidden_units = args[5].shape[2:]
    alone = lax.axis_size("expert") == experts and experts & (experts - 1) == 0
    alone &= hidden_units % CHUNK == 0 and hidden_units > HEAD + CHUNK and CHUNK % BAND == 0
    alone &= hidden_units % (width // 2) == 0 and width % BAND == 0
    return (one_expert_each if alone else shared_experts)(*args)


def solution(mesh):
    in_specs = (
        P("pipe", "expert", None),
        P("expert", None),
        P("pipe", "expert", None),
        P("pipe", None),
        P("pipe", None, None),
        P("pipe", "expert", None, None),
        P("pipe", "expert", None, None),
        P("pipe", "expert", None, None),
    )
    out_specs = P("pipe", "expert", None)
    return jax.shard_map(
        per_device, mesh=mesh, in_specs=in_specs, out_specs=out_specs, check_vma=False
    )
```

```python
import functools

import jax
import jax.numpy as jnp
from jax import lax
from jax.experimental import pallas as pl
from jax.experimental.pallas import tpu as pltpu
from jax.sharding import PartitionSpec as P

MIB = 2**20
CHUNK, BAND = 1024, 512
HEAD = 4096
TERMS = 3
VMEM = pl.BlockSpec(memory_space=pltpu.VMEM)
HBM = pl.BlockSpec(memory_space=pltpu.HBM)


def passed_along(x, axis, by):
    length = lax.axis_size(axis)
    pairs = [(i, i + by) for i in range(length) if 0 <= i + by < length]
    return lax.ppermute(x, axis, pairs)


def swapped(x, k):
    length = lax.axis_size("expert")
    return lax.ppermute(x, "expert", [(i, i ^ k) for i in range(length)])


def slot_hits(routes, experts, capacity, route):
    tokens = routes.shape[1]
    me = lax.axis_index("expert")
    ids = lax.broadcasted_iota(jnp.int32, (experts, tokens), 0) ^ me
    first = (routes[0:1] == ids).astype(jnp.float32)
    second = (routes[1:2] == ids).astype(jnp.float32)
    hits = first + second
    before = lax.broadcasted_iota(jnp.int32, (tokens, tokens), 0) < lax.broadcasted_iota(
        jnp.int32, (tokens, tokens), 1
    )
    rank = jnp.dot(hits, before.astype(jnp.float32), preferred_element_type=jnp.float32)
    slots = lax.broadcasted_iota(jnp.int32, (experts, capacity, tokens), 1).astype(jnp.float32)
    chosen = {0: first, 1: second, None: hits}[route]
    placed = jnp.where(slots == rank[:, None, :], chosen[:, None, :], 0.0)
    return placed.reshape(experts * capacity, tokens)


def normed_rows(values, gain):
    mean_square = jnp.mean(values * values, axis=-1, keepdims=True)
    return (values * lax.rsqrt(mean_square + 1e-05) * gain).astype(jnp.bfloat16)


def tile_comes_late():
    section = lax.axis_index("pipe")
    return (section > 0) & (section < lax.axis_size("pipe") - 1)


def prepare_kernel(
    experts, capacity, fresh, routes, gain, up, placing, fresh_here, routes_here, gain_here, first, sems
):
    pairs = ((routes, routes_here), (fresh, fresh_here), (gain, gain_here))
    copies = [pltpu.make_async_copy(a, b, sems.at[i]) for i, (a, b) in enumerate(pairs)]
    fetch = pltpu.make_async_copy(up.at[:, : first.shape[1]], first, sems.at[len(pairs)])
    for copy in copies:
        copy.start()
    pl.when(tile_comes_late())(fetch.start)
    copies[0].wait()
    placing[...] = slot_hits(routes_here[...], experts, capacity, None).astype(jnp.bfloat16)
    for copy in copies[1:]:
        copy.wait()
    pl.when(tile_comes_late())(fetch.wait)


def pack_kernel(received, fresh, gain, placing, inputs, normed, *blocks):
    section = lax.axis_index("pipe")
    tile = jnp.where(section == 0, fresh[...], received[...])
    inputs[...] = tile
    rows = normed_rows(tile.astype(jnp.float32), gain[...])
    normed[...] = rows
    capacity = blocks[0].shape[0]
    packed = jnp.dot(placing[...], rows, preferred_element_type=jnp.float32).astype(jnp.bfloat16)
    for k, block in enumerate(blocks):
        block[...] = packed[k * capacity : (k + 1) * capacity]


def weigh_kernel(first, head, normed, router, routes, up, weights, rest, sems):
    chunk = first
    fetch = pltpu.make_async_copy(up.at[:, chunk:head], rest.at[:, : head - chunk], sems.at[0])
    fetch.start()
    more = pltpu.make_async_copy(
        up.at[:, head : head + chunk], rest.at[:, head - chunk : head], sems.at[1]
    )
    pl.when(~tile_comes_late())(more.start)
    experts = router.shape[0]
    slots = weights.shape[1]
    logits = lax.dot_general(
        router[...], normed[...], (((1,), (1,)), ((), ())), preferred_element_type=jnp.float32
    )
    tokens = logits.shape[1]
    ids = lax.broadcasted_iota(jnp.int32, (experts, tokens), 0)
    picked = [
        jnp.sum(jnp.where(routes[r : r + 1, :] == ids, logits, 0.0), axis=0, keepdims=True)
        for r in range(2)
    ]
    total = 0.0
    for r in range(2):
        share = jax.nn.sigmoid(picked[r] - picked[1 - r])
        total += slot_hits(routes[...], experts, slots // experts, r) * share
    diagonal = lax.broadcasted_iota(jnp.int32, (slots, slots), 0) == lax.broadcasted_iota(
        jnp.int32, (slots, slots), 1
    )
    for term in range(TERMS):
        part = total.astype(jnp.bfloat16)
        weights[term * tokens : (term + 1) * tokens, :] = lax.dot_general(
            part,
            diagonal.astype(jnp.bfloat16),
            (((0,), (0,)), ((), ())),
            preferred_element_type=jnp.float32,
        ).astype(jnp.bfloat16)
        total = total - part.astype(jnp.float32)
    fetch.wait()
    pl.when(~tile_comes_late())(more.wait)


def first_chunk(c):
    return isinstance(c, int) and c == 0


def ffn_kernel(count, band, head, *refs):
    blocks, (gate, _, _, up, down) = refs[:count], refs[count : count + 5]
    outs, spares = refs[count + 5 : 2 * count + 5], refs[2 * count + 5 : 2 * count + 7]
    rows, hidden, sems, tail_sems = refs[2 * count + 7 :]
    capacity = blocks[0].shape[0]
    width, hidden_units = gate.shape
    chunk = spares[0].shape[1]
    unit = width // 2
    tall = hidden_units // unit
    per_chunk = 2 * chunk // band
    loaded, chunks = head // chunk, hidden_units // chunk
    order = [*range(1, loaded), *range(loaded + 1, chunks), 0, loaded]

    def place(u, c):
        late = int(not first_chunk(c))
        left = (c - 1) * chunk if late else 0
        columns = pl.ds(pl.multiple_of(left + u % per_chunk // 2 * band, band), band)
        return spares[late].at[pl.ds(u % 2 * unit, unit), columns]

    def fetch(u, c):
        source = down.at[pl.ds(u % tall * unit, unit), pl.ds(pl.multiple_of(u // tall * band, band), band)]
        return pltpu.make_async_copy(source, place(u, c), sems.at[u])

    def columns_of(c):
        return pl.ds(pl.multiple_of(c * chunk, chunk), chunk)

    def part_of(c):
        return spares[0] if first_chunk(c) else spares[1].at[:, columns_of(c - 1)]

    def fetch_tail(c, slot):
        return pltpu.make_async_copy(up.at[:, columns_of(c)], part_of(c), tail_sems.at[slot])

    for c in range(loaded + 1, chunks):
        fetch_tail(c, c - loaded).start()
    pl.when(tile_comes_late())(fetch_tail(loaded, 0).start)
    pl.when(~tile_comes_late())(fetch_tail(0, 0).start)
    for k in range(count):
        rows[k * capacity : (k + 1) * capacity, :] = blocks[k][...]

    def step(c, turn):
        x = rows[...]
        gate_proj = jnp.dot(x, gate[:, columns_of(c)], preferred_element_type=jnp.float32)
        up_proj = jnp.dot(x, part_of(c)[...], preferred_element_type=jnp.float32)
        hidden[:, columns_of(c)] = (jax.nn.silu(gate_proj) * up_proj).astype(jnp.bfloat16)
        for j in range(per_chunk):
            fetch(turn * per_chunk + j, c).start()

    @pl.loop(0, loaded - 1)
    def _(turn):
        step(turn + 1, turn)

    @pl.loop(loaded - 1, chunks - 2)
    def _(turn):
        fetch_tail(turn + 2, turn + 2 - loaded).wait()
        step(turn + 2, turn)

    fetch_tail(0, 0).wait()
    step(0, chunks - 2)
    step(loaded, chunks - 1)
    for j in range(width // band):
        total, u = None, j * tall
        last = j == width // band - 1
        if not last:
            for v in range(u, u + tall):
                fetch(v, order[v // per_chunk]).wait()
        while u < (j + 1) * tall:
            paired = u % 2 == 0 and u + 1 < (j + 1) * tall
            c = order[u // per_chunk]
            for v in range(u, u + 1 + paired) if last else ():
                fetch(v, c).wait()
            top, left = u % 2 * unit, u % per_chunk // 2 * band
            part = jnp.dot(
                hidden[:, u % tall * unit : (u % tall + 1 + paired) * unit],
                part_of(c)[top : top + (1 + paired) * unit, left : left + band],
                preferred_element_type=jnp.float32,
            )
            total = part if total is None else total + part
            u += 1 + paired
        for k in range(count):
            outs[k][:, j * band : (j + 1) * band] = total[k * capacity : (k + 1) * capacity].astype(
                jnp.bfloat16
            )


def combine_kernel(order, inputs, weights, *refs):
    blocks, out, back = refs[:-2], refs[-2], refs[-1]
    capacity = blocks[0].shape[0]
    for k, block in zip(order, blocks):
        back[k * capacity : (k + 1) * capacity, :] = block[...]
    terms = jnp.dot(weights[...], back[...], preferred_element_type=jnp.float32)
    total = inputs[...].astype(jnp.float32)
    tokens = total.shape[0]
    for term in range(TERMS):
        total += terms[term * tokens : (term + 1) * tokens]
    out[...] = total.astype(jnp.bfloat16)


def in_vmem(x):
    return pltpu.with_memory_space_constraint(x, pltpu.VMEM)


def in_hbm(x):
    return pltpu.with_memory_space_constraint(x, pltpu.HBM)


def call(kernel, out_shape, in_specs, flops=0, moved=0, limit=2 * MIB, scratch=(), aliases={}):
    return pl.pallas_call(
        kernel,
        out_shape=out_shape,
        in_specs=in_specs,
        out_specs=jax.tree.map(lambda _: VMEM, out_shape),
        scratch_shapes=scratch,
        input_output_aliases=aliases,
        compiler_params=pltpu.CompilerParams(vmem_limit_bytes=limit),
        cost_estimate=pl.CostEstimate(flops=flops, bytes_accessed=moved, transcendentals=0),
    )


def one_expert_each(held, fresh, routes, norm_gain, router, w_gate, w_up, w_down):
    tokens, width = fresh.shape
    experts = router.shape[2]
    capacity = tokens // 2
    slots = experts * capacity
    hidden_units = w_gate.shape[3]
    bf16 = jnp.bfloat16
    chosen = jnp.transpose(routes[0])
    router_rows = jnp.transpose(router[0])
    received = passed_along(held[0], "pipe", 1)
    placing, fresh_here, routes_here, gain_here, up_first = call(
        functools.partial(prepare_kernel, experts, capacity),
        [
            pltpu.VMEM((slots, tokens), bf16),
            pltpu.VMEM(fresh.shape, bf16),
            pltpu.VMEM(chosen.shape, jnp.int32),
            pltpu.VMEM(norm_gain.shape, jnp.float32),
            pltpu.VMEM((width, CHUNK), bf16),
        ],
        [HBM] * 4,
        flops=10**6,
        moved=10**6,
        scratch=[pltpu.SemaphoreType.DMA((4,))],
    )(*map(in_hbm, (fresh, chosen, norm_gain, w_up[0, 0])))
    tile = pltpu.VMEM((tokens, width), bf16)
    block = pltpu.VMEM((capacity, width), bf16)
    inputs, normed, *packed = call(
        pack_kernel, [tile, tile] + [block] * experts, [VMEM] * 4, flops=60 * 10**9, moved=10**6
    )(*map(in_vmem, (received, fresh_here, gain_here, placing)))
    order = range(experts - 1, -1, -1)
    arrived = [swapped(packed[k], k) if k else packed[k] for k in order]
    weights, up_rest = call(
        functools.partial(weigh_kernel, CHUNK, HEAD),
        [pltpu.VMEM((TERMS * tokens, slots), bf16), pltpu.VMEM((width, hidden_units - CHUNK), bf16)],
        [VMEM] * 3 + [HBM],
        flops=10**6,
        moved=2 * width * HEAD,
        scratch=[pltpu.SemaphoreType.DMA((2,))],
    )(in_vmem(normed), router_rows, in_vmem(routes_here), in_hbm(w_up[0, 0]))
    *results, _, _ = call(
        functools.partial(ffn_kernel, experts, BAND, HEAD),
        [block] * experts + [pltpu.VMEM(up.shape, bf16) for up in (up_first, up_rest)],
        [VMEM] * (experts + 3) + [HBM, HBM],
        flops=6 * slots * width * hidden_units,
        moved=6 * width * hidden_units,
        limit=6 * MIB,
        scratch=[
            pltpu.VMEM((slots, width), bf16),
            pltpu.VMEM((slots, hidden_units), bf16),
            pltpu.SemaphoreType.DMA((2 * hidden_units // BAND,)),
            pltpu.SemaphoreType.DMA(((hidden_units - HEAD) // CHUNK,)),
        ],
        aliases={experts + 1: experts, experts + 2: experts + 1},
    )(*map(in_vmem, arrived), *map(in_vmem, (w_gate[0, 0], up_first, up_rest)), *map(in_hbm, (w_up[0, 0], w_down[0, 0])))
    returned = [swapped(result, k) if k else result for result, k in zip(results, order)]
    out = call(
        functools.partial(combine_kernel, order),
        jax.ShapeDtypeStruct((tokens, width), bf16),
        [VMEM] * (experts + 2),
        flops=10**8,
        moved=10**6,
        limit=4 * MIB,
        scratch=[pltpu.VMEM((slots, width), bf16)],
    )(*map(in_vmem, (inputs, weights, *returned)))
    return out[None]


def shared_experts(held, fresh, routes, norm_gain, router, w_gate, w_up, w_down):
    tok_rows = fresh.shape[0]
    model_width = fresh.shape[1]
    experts = router.shape[2]
    devices = lax.axis_size("expert")
    shard_count = devices // experts
    capacity = tok_rows // 2
    received = passed_along(held[0], "pipe", 1)
    section_index = lax.axis_index("pipe")
    inputs = jnp.where(section_index == 0, fresh, received)
    values = inputs.astype(jnp.float32)
    normed = normed_rows(values, norm_gain[0])
    logits = jnp.dot(normed, router[0], preferred_element_type=jnp.float32)
    chosen = routes[0]
    expert_ids = jnp.arange(experts, dtype=jnp.int32)
    token_hits = (chosen[:, :, None] == expert_ids[None, None, :]).astype(jnp.float32)
    picked_logits = jnp.sum(token_hits * logits[:, None, :], axis=2)
    shares = jnp.stack(
        [
            jax.nn.sigmoid(picked_logits[:, 0] - picked_logits[:, 1]),
            jax.nn.sigmoid(picked_logits[:, 1] - picked_logits[:, 0]),
        ],
        axis=1,
    )
    flat_choice = chosen.reshape(-1)
    onehot = (flat_choice[:, None] == expert_ids[None, :]).astype(jnp.int32)
    rank_table = jnp.cumsum(onehot, axis=0) - 1
    slot_index = jnp.sum(onehot * rank_table, axis=1)
    target = flat_choice * capacity + slot_index
    slot_ids = jnp.arange(experts * capacity, dtype=jnp.int32)
    placing = (target[:, None] == slot_ids[None, :]).astype(jnp.bfloat16)
    placing_tok = jnp.sum(placing.reshape(tok_rows, 2, experts * capacity), axis=1)
    buffer = jnp.dot(placing_tok.T, normed, preferred_element_type=jnp.float32).astype(jnp.bfloat16)
    gate_matrix = w_gate[0, 0]
    up_matrix = w_up[0, 0]
    down_matrix = w_down[0, 0]
    outgoing = jnp.broadcast_to(
        buffer.reshape(experts, 1, capacity, model_width),
        (experts, shard_count, capacity, model_width),
    )
    outgoing = outgoing.reshape(devices, capacity, model_width)
    row_block = lax.all_to_all(outgoing, "expert", split_axis=0, concat_axis=0, tiled=True)
    flat_rows = row_block.reshape(-1, model_width)
    gate_proj = jnp.dot(flat_rows, gate_matrix, preferred_element_type=jnp.float32)
    up_proj = jnp.dot(flat_rows, up_matrix, preferred_element_type=jnp.float32)
    hidden = (jax.nn.silu(gate_proj) * up_proj).astype(jnp.bfloat16)
    partial_value = jnp.dot(hidden, down_matrix, preferred_element_type=jnp.float32).astype(
        jnp.bfloat16
    )
    came_back = lax.all_to_all(
        partial_value.reshape(row_block.shape), "expert", split_axis=0, concat_axis=0, tiled=True
    )
    expert_out = jnp.sum(
        came_back.reshape(experts, shard_count, capacity, model_width).astype(jnp.float32), axis=1
    ).astype(jnp.bfloat16)
    picked = jnp.dot(
        placing,
        expert_out.reshape(experts * capacity, model_width),
        preferred_element_type=jnp.float32,
    )
    picked = picked.reshape(tok_rows, 2, model_width)
    branch = shares[:, 0, None] * picked[:, 0] + shares[:, 1, None] * picked[:, 1]
    section_out = (values + branch).astype(jnp.bfloat16)
    return section_out[None]


def per_device(*args):
    experts = args[4].shape[2]
    width, hidden_units = args[5].shape[2:]
    alone = lax.axis_size("expert") == experts and experts & (experts - 1) == 0
    alone &= hidden_units % CHUNK == 0 and hidden_units > HEAD + CHUNK and CHUNK % BAND == 0
    alone &= hidden_units % (width // 2) == 0 and width % BAND == 0
    return (one_expert_each if alone else shared_experts)(*args)


def solution(mesh):
    in_specs = (
        P("pipe", "expert", None),
        P("expert", None),
        P("pipe", "expert", None),
        P("pipe", None),
        P("pipe", None, None),
        P("pipe", "expert", None, None),
        P("pipe", "expert", None, None),
        P("pipe", "expert", None, None),
    )
    out_specs = P("pipe", "expert", None)
    return jax.shard_map(
        per_device, mesh=mesh, in_specs=in_specs, out_specs=out_specs, check_vma=False
    )
```

```python
import functools

import jax
import jax.numpy as jnp
from jax import lax
from jax.experimental import pallas as pl
from jax.experimental.pallas import tpu as pltpu
from jax.sharding import PartitionSpec as P

MIB = 2**20
CHUNK, BAND = 1024, 512
HEAD = 4096
TERMS = 3
VMEM = pl.BlockSpec(memory_space=pltpu.VMEM)
HBM = pl.BlockSpec(memory_space=pltpu.HBM)


def passed_along(x, axis, by):
    length = lax.axis_size(axis)
    pairs = [(i, i + by) for i in range(length) if 0 <= i + by < length]
    return lax.ppermute(x, axis, pairs)


def swapped(x, k):
    length = lax.axis_size("expert")
    return lax.ppermute(x, "expert", [(i, i ^ k) for i in range(length)])


def slot_hits(routes, experts, capacity, route):
    tokens = routes.shape[1]
    me = lax.axis_index("expert")
    ids = lax.broadcasted_iota(jnp.int32, (experts, tokens), 0) ^ me
    first = (routes[0:1] == ids).astype(jnp.float32)
    second = (routes[1:2] == ids).astype(jnp.float32)
    hits = first + second
    before = lax.broadcasted_iota(jnp.int32, (tokens, tokens), 0) < lax.broadcasted_iota(
        jnp.int32, (tokens, tokens), 1
    )
    rank = jnp.dot(hits, before.astype(jnp.float32), preferred_element_type=jnp.float32)
    slots = lax.broadcasted_iota(jnp.int32, (experts, capacity, tokens), 1).astype(jnp.float32)
    chosen = {0: first, 1: second, None: hits}[route]
    placed = jnp.where(slots == rank[:, None, :], chosen[:, None, :], 0.0)
    return placed.reshape(experts * capacity, tokens)


def normed_rows(values, gain):
    mean_square = jnp.mean(values * values, axis=-1, keepdims=True)
    return (values * lax.rsqrt(mean_square + 1e-05) * gain).astype(jnp.bfloat16)


def tile_comes_late():
    section = lax.axis_index("pipe")
    return (section > 1) & (section < lax.axis_size("pipe") - 1)


def prepare_kernel(
    experts, capacity, fresh, routes, gain, up, placing, fresh_here, routes_here, gain_here, first, sems
):
    pairs = ((routes, routes_here), (fresh, fresh_here), (gain, gain_here))
    copies = [pltpu.make_async_copy(a, b, sems.at[i]) for i, (a, b) in enumerate(pairs)]
    fetch = pltpu.make_async_copy(up.at[:, : first.shape[1]], first, sems.at[len(pairs)])
    for copy in copies:
        copy.start()
    pl.when(tile_comes_late())(fetch.start)
    copies[0].wait()
    placing[...] = slot_hits(routes_here[...], experts, capacity, None).astype(jnp.bfloat16)
    for copy in copies[1:]:
        copy.wait()
    pl.when(tile_comes_late())(fetch.wait)


def pack_kernel(received, fresh, gain, placing, inputs, normed, *blocks):
    section = lax.axis_index("pipe")
    tile = jnp.where(section == 0, fresh[...], received[...])
    inputs[...] = tile
    rows = normed_rows(tile.astype(jnp.float32), gain[...])
    normed[...] = rows
    capacity = blocks[0].shape[0]
    packed = jnp.dot(placing[...], rows, preferred_element_type=jnp.float32).astype(jnp.bfloat16)
    for k, block in enumerate(blocks):
        block[...] = packed[k * capacity : (k + 1) * capacity]


def weigh_kernel(first, head, normed, router, routes, up, weights, rest, sems):
    chunk = first
    fetch = pltpu.make_async_copy(up.at[:, chunk:head], rest.at[:, : head - chunk], sems.at[0])
    fetch.start()
    more = pltpu.make_async_copy(
        up.at[:, head : head + chunk], rest.at[:, head - chunk : head], sems.at[1]
    )
    pl.when(~tile_comes_late())(more.start)
    experts = router.shape[0]
    slots = weights.shape[1]
    logits = lax.dot_general(
        router[...], normed[...], (((1,), (1,)), ((), ())), preferred_element_type=jnp.float32
    )
    tokens = logits.shape[1]
    ids = lax.broadcasted_iota(jnp.int32, (experts, tokens), 0)
    picked = [
        jnp.sum(jnp.where(routes[r : r + 1, :] == ids, logits, 0.0), axis=0, keepdims=True)
        for r in range(2)
    ]
    total = 0.0
    for r in range(2):
        share = jax.nn.sigmoid(picked[r] - picked[1 - r])
        total += slot_hits(routes[...], experts, slots // experts, r) * share
    diagonal = lax.broadcasted_iota(jnp.int32, (slots, slots), 0) == lax.broadcasted_iota(
        jnp.int32, (slots, slots), 1
    )
    for term in range(TERMS):
        part = total.astype(jnp.bfloat16)
        weights[term * tokens : (term + 1) * tokens, :] = lax.dot_general(
            part,
            diagonal.astype(jnp.bfloat16),
            (((0,), (0,)), ((), ())),
            preferred_element_type=jnp.float32,
        ).astype(jnp.bfloat16)
        total = total - part.astype(jnp.float32)
    fetch.wait()
    pl.when(~tile_comes_late())(more.wait)


def first_chunk(c):
    return isinstance(c, int) and c == 0


def ffn_kernel(count, band, head, *refs):
    blocks, (gate, _, _, up, down) = refs[:count], refs[count : count + 5]
    outs, spares = refs[count + 5 : 2 * count + 5], refs[2 * count + 5 : 2 * count + 7]
    rows, hidden, sems, tail_sems = refs[2 * count + 7 :]
    capacity = blocks[0].shape[0]
    width, hidden_units = gate.shape
    chunk = spares[0].shape[1]
    unit = width // 2
    tall = hidden_units // unit
    per_chunk = 2 * chunk // band
    loaded, chunks = head // chunk, hidden_units // chunk
    order = [*range(1, loaded), *range(loaded + 1, chunks), 0, loaded]

    def place(u, c):
        late = int(not first_chunk(c))
        left = (c - 1) * chunk if late else 0
        columns = pl.ds(pl.multiple_of(left + u % per_chunk // 2 * band, band), band)
        return spares[late].at[pl.ds(u % 2 * unit, unit), columns]

    def fetch(u, c):
        source = down.at[pl.ds(u % tall * unit, unit), pl.ds(pl.multiple_of(u // tall * band, band), band)]
        return pltpu.make_async_copy(source, place(u, c), sems.at[u])

    def columns_of(c):
        return pl.ds(pl.multiple_of(c * chunk, chunk), chunk)

    def part_of(c):
        return spares[0] if first_chunk(c) else spares[1].at[:, columns_of(c - 1)]

    def fetch_tail(c, slot):
        return pltpu.make_async_copy(up.at[:, columns_of(c)], part_of(c), tail_sems.at[slot])

    for c in range(loaded + 1, chunks):
        fetch_tail(c, c - loaded).start()
    pl.when(tile_comes_late())(fetch_tail(loaded, 0).start)
    pl.when(~tile_comes_late())(fetch_tail(0, 0).start)
    for k in range(count):
        rows[k * capacity : (k + 1) * capacity, :] = blocks[k][...]

    def step(c, turn):
        x = rows[...]
        gate_proj = jnp.dot(x, gate[:, columns_of(c)], preferred_element_type=jnp.float32)
        up_proj = jnp.dot(x, part_of(c)[...], preferred_element_type=jnp.float32)
        hidden[:, columns_of(c)] = (jax.nn.silu(gate_proj) * up_proj).astype(jnp.bfloat16)
        for j in range(per_chunk):
            fetch(turn * per_chunk + j, c).start()

    @pl.loop(0, loaded - 1)
    def _(turn):
        step(turn + 1, turn)

    @pl.loop(loaded - 1, chunks - 2)
    def _(turn):
        fetch_tail(turn + 2, turn + 2 - loaded).wait()
        step(turn + 2, turn)

    fetch_tail(0, 0).wait()
    step(0, chunks - 2)
    step(loaded, chunks - 1)
    for j in range(width // band):
        total, u = None, j * tall
        last = j == width // band - 1
        if not last:
            for v in range(u, u + tall):
                fetch(v, order[v // per_chunk]).wait()
        while u < (j + 1) * tall:
            paired = u % 2 == 0 and u + 1 < (j + 1) * tall
            c = order[u // per_chunk]
            for v in range(u, u + 1 + paired) if last else ():
                fetch(v, c).wait()
            top, left = u % 2 * unit, u % per_chunk // 2 * band
            part = jnp.dot(
                hidden[:, u % tall * unit : (u % tall + 1 + paired) * unit],
                part_of(c)[top : top + (1 + paired) * unit, left : left + band],
                preferred_element_type=jnp.float32,
            )
            total = part if total is None else total + part
            u += 1 + paired
        for k in range(count):
            outs[k][:, j * band : (j + 1) * band] = total[k * capacity : (k + 1) * capacity].astype(
                jnp.bfloat16
            )


def combine_kernel(order, inputs, weights, *refs):
    blocks, out, back = refs[:-2], refs[-2], refs[-1]
    capacity = blocks[0].shape[0]
    for k, block in zip(order, blocks):
        back[k * capacity : (k + 1) * capacity, :] = block[...]
    terms = jnp.dot(weights[...], back[...], preferred_element_type=jnp.float32)
    total = inputs[...].astype(jnp.float32)
    tokens = total.shape[0]
    for term in range(TERMS):
        total += terms[term * tokens : (term + 1) * tokens]
    out[...] = total.astype(jnp.bfloat16)


def in_vmem(x):
    return pltpu.with_memory_space_constraint(x, pltpu.VMEM)


def in_hbm(x):
    return pltpu.with_memory_space_constraint(x, pltpu.HBM)


def call(kernel, out_shape, in_specs, flops=0, moved=0, limit=2 * MIB, scratch=(), aliases={}):
    return pl.pallas_call(
        kernel,
        out_shape=out_shape,
        in_specs=in_specs,
        out_specs=jax.tree.map(lambda _: VMEM, out_shape),
        scratch_shapes=scratch,
        input_output_aliases=aliases,
        compiler_params=pltpu.CompilerParams(vmem_limit_bytes=limit),
        cost_estimate=pl.CostEstimate(flops=flops, bytes_accessed=moved, transcendentals=0),
    )


def one_expert_each(held, fresh, routes, norm_gain, router, w_gate, w_up, w_down):
    tokens, width = fresh.shape
    experts = router.shape[2]
    capacity = tokens // 2
    slots = experts * capacity
    hidden_units = w_gate.shape[3]
    bf16 = jnp.bfloat16
    chosen = jnp.transpose(routes[0])
    router_rows = jnp.transpose(router[0])
    received = passed_along(held[0], "pipe", 1)
    placing, fresh_here, routes_here, gain_here, up_first = call(
        functools.partial(prepare_kernel, experts, capacity),
        [
            pltpu.VMEM((slots, tokens), bf16),
            pltpu.VMEM(fresh.shape, bf16),
            pltpu.VMEM(chosen.shape, jnp.int32),
            pltpu.VMEM(norm_gain.shape, jnp.float32),
            pltpu.VMEM((width, CHUNK), bf16),
        ],
        [HBM] * 4,
        flops=10**6,
        moved=10**6,
        scratch=[pltpu.SemaphoreType.DMA((4,))],
    )(*map(in_hbm, (fresh, chosen, norm_gain, w_up[0, 0])))
    tile = pltpu.VMEM((tokens, width), bf16)
    block = pltpu.VMEM((capacity, width), bf16)
    inputs, normed, *packed = call(
        pack_kernel, [tile, tile] + [block] * experts, [VMEM] * 4, flops=60 * 10**9, moved=10**6
    )(*map(in_vmem, (received, fresh_here, gain_here, placing)))
    order = range(experts - 1, -1, -1)
    arrived = [swapped(packed[k], k) if k else packed[k] for k in order]
    weights, up_rest = call(
        functools.partial(weigh_kernel, CHUNK, HEAD),
        [pltpu.VMEM((TERMS * tokens, slots), bf16), pltpu.VMEM((width, hidden_units - CHUNK), bf16)],
        [VMEM] * 3 + [HBM],
        flops=10**6,
        moved=2 * width * HEAD,
        scratch=[pltpu.SemaphoreType.DMA((2,))],
    )(in_vmem(normed), router_rows, in_vmem(routes_here), in_hbm(w_up[0, 0]))
    *results, _, _ = call(
        functools.partial(ffn_kernel, experts, BAND, HEAD),
        [block] * experts + [pltpu.VMEM(up.shape, bf16) for up in (up_first, up_rest)],
        [VMEM] * (experts + 3) + [HBM, HBM],
        flops=6 * slots * width * hidden_units,
        moved=6 * width * hidden_units,
        limit=6 * MIB,
        scratch=[
            pltpu.VMEM((slots, width), bf16),
            pltpu.VMEM((slots, hidden_units), bf16),
            pltpu.SemaphoreType.DMA((2 * hidden_units // BAND,)),
            pltpu.SemaphoreType.DMA(((hidden_units - HEAD) // CHUNK,)),
        ],
        aliases={experts + 1: experts, experts + 2: experts + 1},
    )(*map(in_vmem, arrived), *map(in_vmem, (w_gate[0, 0], up_first, up_rest)), *map(in_hbm, (w_up[0, 0], w_down[0, 0])))
    returned = [swapped(result, k) if k else result for result, k in zip(results, order)]
    out = call(
        functools.partial(combine_kernel, order),
        jax.ShapeDtypeStruct((tokens, width), bf16),
        [VMEM] * (experts + 2),
        flops=10**8,
        moved=10**6,
        limit=4 * MIB,
        scratch=[pltpu.VMEM((slots, width), bf16)],
    )(*map(in_vmem, (inputs, weights, *returned)))
    return out[None]


def shared_experts(held, fresh, routes, norm_gain, router, w_gate, w_up, w_down):
    tok_rows = fresh.shape[0]
    model_width = fresh.shape[1]
    experts = router.shape[2]
    devices = lax.axis_size("expert")
    shard_count = devices // experts
    capacity = tok_rows // 2
    received = passed_along(held[0], "pipe", 1)
    section_index = lax.axis_index("pipe")
    inputs = jnp.where(section_index == 0, fresh, received)
    values = inputs.astype(jnp.float32)
    normed = normed_rows(values, norm_gain[0])
    logits = jnp.dot(normed, router[0], preferred_element_type=jnp.float32)
    chosen = routes[0]
    expert_ids = jnp.arange(experts, dtype=jnp.int32)
    token_hits = (chosen[:, :, None] == expert_ids[None, None, :]).astype(jnp.float32)
    picked_logits = jnp.sum(token_hits * logits[:, None, :], axis=2)
    shares = jnp.stack(
        [
            jax.nn.sigmoid(picked_logits[:, 0] - picked_logits[:, 1]),
            jax.nn.sigmoid(picked_logits[:, 1] - picked_logits[:, 0]),
        ],
        axis=1,
    )
    flat_choice = chosen.reshape(-1)
    onehot = (flat_choice[:, None] == expert_ids[None, :]).astype(jnp.int32)
    rank_table = jnp.cumsum(onehot, axis=0) - 1
    slot_index = jnp.sum(onehot * rank_table, axis=1)
    target = flat_choice * capacity + slot_index
    slot_ids = jnp.arange(experts * capacity, dtype=jnp.int32)
    placing = (target[:, None] == slot_ids[None, :]).astype(jnp.bfloat16)
    placing_tok = jnp.sum(placing.reshape(tok_rows, 2, experts * capacity), axis=1)
    buffer = jnp.dot(placing_tok.T, normed, preferred_element_type=jnp.float32).astype(jnp.bfloat16)
    gate_matrix = w_gate[0, 0]
    up_matrix = w_up[0, 0]
    down_matrix = w_down[0, 0]
    outgoing = jnp.broadcast_to(
        buffer.reshape(experts, 1, capacity, model_width),
        (experts, shard_count, capacity, model_width),
    )
    outgoing = outgoing.reshape(devices, capacity, model_width)
    row_block = lax.all_to_all(outgoing, "expert", split_axis=0, concat_axis=0, tiled=True)
    flat_rows = row_block.reshape(-1, model_width)
    gate_proj = jnp.dot(flat_rows, gate_matrix, preferred_element_type=jnp.float32)
    up_proj = jnp.dot(flat_rows, up_matrix, preferred_element_type=jnp.float32)
    hidden = (jax.nn.silu(gate_proj) * up_proj).astype(jnp.bfloat16)
    partial_value = jnp.dot(hidden, down_matrix, preferred_element_type=jnp.float32).astype(
        jnp.bfloat16
    )
    came_back = lax.all_to_all(
        partial_value.reshape(row_block.shape), "expert", split_axis=0, concat_axis=0, tiled=True
    )
    expert_out = jnp.sum(
        came_back.reshape(experts, shard_count, capacity, model_width).astype(jnp.float32), axis=1
    ).astype(jnp.bfloat16)
    picked = jnp.dot(
        placing,
        expert_out.reshape(experts * capacity, model_width),
        preferred_element_type=jnp.float32,
    )
    picked = picked.reshape(tok_rows, 2, model_width)
    branch = shares[:, 0, None] * picked[:, 0] + shares[:, 1, None] * picked[:, 1]
    section_out = (values + branch).astype(jnp.bfloat16)
    return section_out[None]


def per_device(*args):
    experts = args[4].shape[2]
    width, hidden_units = args[5].shape[2:]
    alone = lax.axis_size("expert") == experts and experts & (experts - 1) == 0
    alone &= hidden_units % CHUNK == 0 and hidden_units > HEAD + CHUNK and CHUNK % BAND == 0
    alone &= hidden_units % (width // 2) == 0 and width % BAND == 0
    return (one_expert_each if alone else shared_experts)(*args)


def solution(mesh):
    in_specs = (
        P("pipe", "expert", None),
        P("expert", None),
        P("pipe", "expert", None),
        P("pipe", None),
        P("pipe", None, None),
        P("pipe", "expert", None, None),
        P("pipe", "expert", None, None),
        P("pipe", "expert", None, None),
    )
    out_specs = P("pipe", "expert", None)
    return jax.shard_map(
        per_device, mesh=mesh, in_specs=in_specs, out_specs=out_specs, check_vma=False
    )
```
